32 devices in a mesh: peer: 4 (over x, core), fsdp: 8 (over z, y).
Axes of the slice: x: 2, y: 2, z: 4, core: 2. Of those that a mesh axis runs over, the one named last changes fastest.
Arguments:
- tokens: bfloat16 [4, 1024, 2048], P('peer', 'fsdp'), may hold values from -6 to 6
- gate_weight: bfloat16 [4, 5632, 2048], P('peer', 'fsdp'), may hold values from -6 to 6
- up_weight: bfloat16 [4, 5632, 2048], P('peer', 'fsdp'), may hold values from -6 to 6
- down_weight: bfloat16 [4, 5632, 2048], P('peer', 'fsdp'), may hold values from -6 to 6
- cotangent: bfloat16 [4, 1024, 2048], P('peer', 'fsdp'), may hold values from -6 to 6
Outputs:
- new_gate: bfloat16 [4, 5632, 2048], P('peer', 'fsdp')
- new_up: bfloat16 [4, 5632, 2048], P('peer', 'fsdp')
The draws below stay inside these ranges and needn't reach their ends.
All inputs are finite; a program needn't handle non-finite values.
Results may differ from the reference program's by a relative error of at most 0.0054.
Values may be sent and summed in bfloat16 or wider, within the bound.
A program may use at most 128 MiB of HBM per device.

```python
import jax
import jax.numpy as jnp
from jax import lax

D = 2048
FF = 5632
HOP = 2
GROUPS = 4
TOK_GROUP = 1024


def block_levels(stream_key, extent, pieces, smallest, top_value):
    def one(position, blocks):
        heights = jax.random.uniform(jax.random.fold_in(jax.random.fold_in(stream_key, 6), position), (blocks,), jnp.float32, smallest / len(pieces), top_value / len(pieces))
        return jnp.repeat(jnp.exp(heights), extent[position] // blocks).reshape((-1,) + (1,) * (len(extent) - position - 1))

    level = one(*pieces[0])
    for cut in pieces[1:]:
        level = level * one(*cut)
    return level


def scatter_about(own_key, dims, scale, reach, pieces=(), held_as=jnp.bfloat16):
    loudness = block_levels(own_key, dims, pieces, -0.22, 0.18) if pieces else 1.0
    values = jax.random.normal(own_key, dims, jnp.float32) * scale * loudness
    return jnp.minimum(jnp.maximum(values, -reach), reach).astype(held_as)


def setup_inputs(seed: int = 0) -> dict:
    key_of = jax.random.split(jax.random.key(seed), 6)
    return {
        "tokens": scatter_about(key_of[0], (GROUPS, TOK_GROUP, D), 1.0, 6.0, ((0, 4), (1, 8))),
        "gate_weight": scatter_about(key_of[1], (GROUPS, FF, D), 1.0, 6.0, ((0, 4), (1, 8))),
        "up_weight": scatter_about(key_of[2], (GROUPS, FF, D), 1.0, 6.0, ((0, 4), (1, 8))),
        "down_weight": scatter_about(key_of[3], (GROUPS, FF, D), 1.0, 6.0, ((0, 4), (1, 8))),
        "cotangent": scatter_about(key_of[4], (GROUPS, TOK_GROUP, D), 1.0, 6.0, ((0, 4), (1, 8))),
    }


rate_value = 1.0


def group_step(operands):
    tokens_in, gate_in, up_in, down_in, cotangent_in = operands
    gate = jnp.dot(tokens_in, gate_in.T, preferred_element_type=jnp.float32) * (D ** -0.5)
    upper = jnp.dot(tokens_in, up_in.T, preferred_element_type=jnp.float32) * (D ** -0.5)
    dhidden = jnp.dot(cotangent_in, down_in.T, preferred_element_type=jnp.float32) * (FF ** -0.5)
    sigma = jax.nn.sigmoid(gate)
    dgate = (dhidden * upper * sigma * (1.0 + gate * (1.0 - sigma))).astype(jnp.bfloat16)
    dupper = (dhidden * gate * sigma).astype(jnp.bfloat16)
    grad_gate = jnp.dot(dgate.T, tokens_in, preferred_element_type=jnp.float32) * (D ** -0.5)
    grad_upper = jnp.dot(dupper.T, tokens_in, preferred_element_type=jnp.float32) * (D ** -0.5)
    stepped_gate = (gate_in.astype(jnp.float32) - rate_value * grad_gate).astype(jnp.bfloat16)
    stepped_upper = (up_in.astype(jnp.float32) - rate_value * grad_upper).astype(jnp.bfloat16)
    return stepped_gate, stepped_upper


def reference(tokens, gate_weight, up_weight, down_weight, cotangent):
    stepped_gate, stepped_upper = lax.map(group_step, (tokens, gate_weight, up_weight, down_weight, cotangent))
    partner_gate = jnp.roll(stepped_gate, HOP, axis=0)
    partner_upper = jnp.roll(stepped_upper, HOP, axis=0)
    new_gate = ((stepped_gate.astype(jnp.float32) + partner_gate.astype(jnp.float32)) * 0.5).astype(jnp.bfloat16)
    new_up = ((stepped_upper.astype(jnp.float32) + partner_upper.astype(jnp.float32)) * 0.5).astype(jnp.bfloat16)
    return new_gate, new_up
```

```python
import functools

import jax
import jax.numpy as jnp
from jax import lax
from jax.experimental import pallas as pl
from jax.experimental.pallas import tpu as pltpu
from jax.sharding import PartitionSpec as P

HOP = 2
CHUNKS = 11
RATE = 1.0
MESH = pl.DeviceIdType.MESH


def nt(left, right):
    return lax.dot_general(
        left, right, (((1,), (1,)), ((), ())), preferred_element_type=jnp.float32
    )


def kernel(
    fsdp,
    peers,
    tok_in,
    gate_in,
    up_in,
    down_in,
    cot_in,
    gate_out,
    up_out,
    tok,
    cot,
    wg,
    wu,
    wd,
    dgate,
    dup,
    own,
    landed,
    load_sem,
    send_sem,
    recv_sem,
    peer_send,
    peer_recv,
    out_sem,
):
    part, width = tok_in.shape[1], tok_in.shape[2]
    rows = gate_in.shape[1]
    chunk = rows // CHUNKS
    in_scale = width ** (-0.5)
    hidden_scale = (rows * fsdp) ** (-0.5)
    deep = fsdp // 2

    me = lax.axis_index("fsdp")
    peer = lax.axis_index("peer")
    z, y = me // 2, me % 2
    across = z * 2 + 1 - y
    to_peer = lax.rem(peer + HOP, peers)
    from_peer = lax.rem(peer + peers - HOP, peers)
    has_prev, has_next = z > 0, z < deep - 1

    ins = (tok_in, cot_in)
    bufs = (tok, cot)

    loads = [
        pltpu.make_async_copy(source.at[0], target, load_sem.at[k])
        for k, (source, target) in enumerate(((gate_in, wg), (up_in, wu), (down_in, wd)))
    ]

    def span(origin):
        return pl.ds(pl.multiple_of(origin * part, part), part)

    loads += [
        pltpu.make_async_copy(ins[a].at[0], bufs[a].at[span(me), :], load_sem.at[3 + a])
        for a in range(2)
    ]
    for load in reversed(loads):
        load.start()

    barrier = pltpu.get_barrier_semaphore()

    def greet(target):
        pl.semaphore_signal(barrier, inc=1, device_id=target, device_id_type=MESH)

    greet({"fsdp": across})
    greet({"peer": to_peer})
    greet({"peer": from_peer})

    @pl.when(has_prev)
    def _():
        greet({"fsdp": me - 2})

    @pl.when(has_next)
    def _():
        greet({"fsdp": me + 2})

    pl.semaphore_wait(barrier, 3 + has_prev.astype(jnp.int32) + has_next.astype(jnp.int32))

    def hop(a, origin, way, first=False):
        target = (me + 2, me - 2, across)[way]
        here = bufs[a].at[span(origin), :]
        return pltpu.make_async_remote_copy(
            src_ref=ins[a].at[0] if first else here,
            dst_ref=here,
            send_sem=send_sem.at[a, origin, way],
            recv_sem=recv_sem.at[a, origin],
            device_id={"fsdp": target},
            device_id_type=MESH,
        )

    def arrive(a, origin):
        hop(a, origin, 2).wait_recv()

    for a in range(2):
        @pl.when(has_next)
        def _():
            hop(a, me, 0, True).start()

        @pl.when(has_prev)
        def _():
            hop(a, me, 1, True).start()

        hop(a, me, 2, True).start()

    def forward(origin):
        lanes = span(origin)
        half = rows // 2

        def some(i, carry):
            at = pl.ds(pl.multiple_of(i * half, half), half)
            gate = nt(wg[at, :], tok[lanes, :]) * in_scale
            upper = nt(wu[at, :], tok[lanes, :]) * in_scale
            dhidden = nt(wd[at, :], cot[lanes, :]) * hidden_scale
            sigma = jax.nn.sigmoid(gate)
            dgate[at, lanes] = (
                dhidden * upper * sigma * (1.0 + gate * (1.0 - sigma))
            ).astype(jnp.bfloat16)
            dup[at, lanes] = (dhidden * gate * sigma).astype(jnp.bfloat16)
            return carry

        lax.fori_loop(0, 2, some, 0)

    for load in loads:
        load.wait()
    forward(me)

    for step in range(1, deep + 1):
        left, right = me - 2 * step, me + 2 * step
        has_left, has_right = z - step >= 0, z + step < deep
        near_left, near_right = across - 2 * (step - 1), across + 2 * (step - 1)
        has_near_left, has_near_right = z - step + 1 >= 0, z + step - 1 < deep
        for a in range(2):
            if step < deep:
                @pl.when(has_left)
                def _():
                    arrive(a, left)

                    @pl.when(has_next)
                    def _():
                        hop(a, left, 0).start()

                    hop(a, left, 2).start()

                @pl.when(has_right)
                def _():
                    arrive(a, right)

                    @pl.when(has_prev)
                    def _():
                        hop(a, right, 1).start()

                    hop(a, right, 2).start()

        if step < deep:
            @pl.when(has_left)
            def _():
                forward(left)

            @pl.when(has_right)
            def _():
                forward(right)

        @pl.when(has_near_left)
        def _():
            for a in range(2):
                arrive(a, near_left)
            forward(near_left)

        if step > 1:
            @pl.when(has_near_right)
            def _():
                for a in range(2):
                    arrive(a, near_right)
                forward(near_right)

    def rows_of(c):
        return pl.ds(pl.multiple_of(c * chunk, chunk), chunk)

    def exchange(c):
        return pltpu.make_async_remote_copy(
            src_ref=own.at[c],
            dst_ref=landed.at[c],
            send_sem=peer_send.at[c],
            recv_sem=peer_recv.at[c],
            device_id={"peer": to_peer},
            device_id_type=MESH,
        )

    def update(c, carry):
        at = rows_of(c)
        grad = jnp.dot(
            jnp.concatenate([dgate[at, :], dup[at, :]], axis=0),
            tok[...],
            preferred_element_type=jnp.float32,
        ) * in_scale
        weight = jnp.concatenate([wg[at, :], wu[at, :]], axis=0).astype(jnp.float32)
        own[c] = (weight - RATE * grad).astype(jnp.bfloat16)
        exchange(c).start()
        return carry

    lax.fori_loop(0, CHUNKS, update, 0)

    def results(c):
        at = rows_of(c)
        return (
            pltpu.make_async_copy(
                landed.at[c, pl.ds(0, chunk), :], gate_out.at[0, at, :], out_sem.at[0, c]
            ),
            pltpu.make_async_copy(
                landed.at[c, pl.ds(chunk, chunk), :], up_out.at[0, at, :], out_sem.at[1, c]
            ),
        )

    def average(c, carry):
        exchange(c).wait_recv()
        landed[c] = (
            (own[c].astype(jnp.float32) + landed[c].astype(jnp.float32)) * 0.5
        ).astype(jnp.bfloat16)
        for copy in results(c):
            copy.start()
        return carry

    lax.fori_loop(0, CHUNKS, average, 0)

    def finish(c, carry):
        exchange(c).wait_send()
        for copy in results(c):
            copy.wait()
        return carry

    lax.fori_loop(0, CHUNKS, finish, 0)

    for a in range(2):
        for step in range(deep):
            left, right = me - 2 * step, me + 2 * step

            @pl.when(z - step >= 0)
            def _():
                @pl.when(has_next)
                def _():
                    hop(a, left, 0).wait_send()

                hop(a, left, 2).wait_send()

            @pl.when(z + step < deep)
            def _():
                @pl.when(has_prev)
                def _():
                    hop(a, right, 1).wait_send()

                if step > 0:
                    hop(a, right, 2).wait_send()


def solution(mesh):
    fsdp, peers = mesh.shape["fsdp"], mesh.shape["peer"]

    def body(tokens, gate_weight, up_weight, down_weight, cotangent):
        _, part, width = tokens.shape
        rows = gate_weight.shape[1]
        every = part * fsdp
        bf16 = jnp.bfloat16
        result = jax.ShapeDtypeStruct((1, rows, width), bf16)
        flops = 10 * every * rows * width
        return pl.pallas_call(
            functools.partial(kernel, fsdp, peers),
            out_shape=(result, result),
            in_specs=[pl.BlockSpec(memory_space=pl.ANY)] * 5,
            out_specs=(pl.BlockSpec(memory_space=pl.ANY),) * 2,
            scratch_shapes=[
                pltpu.VMEM((every, width), bf16),
                pltpu.VMEM((every, width), bf16),
                pltpu.VMEM((rows, width), bf16),
                pltpu.VMEM((rows, width), bf16),
                pltpu.VMEM((rows, width), bf16),
                pltpu.VMEM((rows, every), bf16),
                pltpu.VMEM((rows, every), bf16),
                pltpu.VMEM((CHUNKS, 2 * rows // CHUNKS, width), bf16),
                pltpu.VMEM((CHUNKS, 2 * rows // CHUNKS, width), bf16),
                pltpu.SemaphoreType.DMA((5,)),
                pltpu.SemaphoreType.DMA((2, fsdp, 3)),
                pltpu.SemaphoreType.DMA((2, fsdp)),
                pltpu.SemaphoreType.DMA((CHUNKS,)),
                pltpu.SemaphoreType.DMA((CHUNKS,)),
                pltpu.SemaphoreType.DMA((2, CHUNKS)),
            ],
            compiler_params=pltpu.CompilerParams(
                collective_id=0, has_side_effects=True, vmem_limit_bytes=56 * 2**20
            ),
            cost_estimate=pl.CostEstimate(
                flops=flops, bytes_accessed=10 * rows * width, transcendentals=every * rows
            ),
        )(tokens, gate_weight, up_weight, down_weight, cotangent)

    spec = P("peer", "fsdp", None)
    return jax.shard_map(
        body, mesh=mesh, in_specs=(spec,) * 5, out_specs=(spec, spec), check_vma=False
    )
```

```python
import functools

import jax
import jax.numpy as jnp
from jax import lax
from jax.experimental import pallas as pl
from jax.experimental.pallas import tpu as pltpu
from jax.sharding import PartitionSpec as P

HOP = 2
CHUNKS = 11
EARLY = 5
LATE = CHUNKS - EARLY
RATE = 1.0
MESH = pl.DeviceIdType.MESH


def nt(left, right):
    return lax.dot_general(
        left, right, (((1,), (1,)), ((), ())), preferred_element_type=jnp.float32
    )


def kernel(
    fsdp,
    peers,
    tok_in,
    gate_in,
    up_in,
    down_in,
    cot_in,
    gate_out,
    up_out,
    tok,
    cot,
    wg,
    wu,
    wd,
    tok_theirs,
    dhid,
    dhid_theirs,
    weight_theirs,
    own,
    landed,
    load_sem,
    send_sem,
    recv_sem,
    peer_send,
    peer_recv,
    raw_send,
    raw_recv,
    dhid_send,
    dhid_recv,
    out_sem,
):
    part, width = tok_in.shape[1], tok_in.shape[2]
    rows = gate_in.shape[1]
    chunk = rows // CHUNKS
    in_scale = width ** (-0.5)
    hidden_scale = (rows * fsdp) ** (-0.5)
    deep = fsdp // 2

    me = lax.axis_index("fsdp")
    peer = lax.axis_index("peer")
    z, y = me // 2, me % 2
    across = z * 2 + 1 - y
    to_peer = lax.rem(peer + HOP, peers)
    from_peer = lax.rem(peer + peers - HOP, peers)
    has_prev, has_next = z > 0, z < deep - 1

    ins = (tok_in, cot_in)
    bufs = (tok, cot, tok_theirs)
    early_rows = pl.ds(LATE * chunk, EARLY * chunk)

    loads = [
        pltpu.make_async_copy(source.at[0], target, load_sem.at[k])
        for k, (source, target) in enumerate(((gate_in, wg), (up_in, wu), (down_in, wd)))
    ]

    def span(origin):
        return pl.ds(pl.multiple_of(origin * part, part), part)

    loads += [
        pltpu.make_async_copy(ins[a].at[0], bufs[a].at[span(me), :], load_sem.at[3 + a])
        for a in range(2)
    ]
    for load in reversed(loads):
        load.start()

    barrier = pltpu.get_barrier_semaphore()

    def greet(target):
        pl.semaphore_signal(barrier, inc=1, device_id=target, device_id_type=MESH)

    greet({"fsdp": across})
    greet({"peer": to_peer})
    greet({"peer": from_peer})

    @pl.when(has_prev)
    def _():
        greet({"fsdp": me - 2})

    @pl.when(has_next)
    def _():
        greet({"fsdp": me + 2})

    pl.semaphore_wait(barrier, 3 + has_prev.astype(jnp.int32) + has_next.astype(jnp.int32))

    def hop(a, origin, way, first=False):
        target = (me + 2, me - 2, across)[way]
        here = bufs[a].at[span(origin), :]
        return pltpu.make_async_remote_copy(
            src_ref=ins[a].at[0] if first else here,
            dst_ref=here,
            send_sem=send_sem.at[a, origin, way],
            recv_sem=recv_sem.at[a, origin],
            device_id={"fsdp": target},
            device_id_type=MESH,
        )

    def arrive(a, origin):
        hop(a, origin, 2).wait_recv()

    def first_hops(a, first):
        @pl.when(has_next)
        def _():
            hop(a, me, 0, first).start()

        @pl.when(has_prev)
        def _():
            hop(a, me, 1, first).start()

        hop(a, me, 2, first).start()

    for a in range(2):
        first_hops(a, True)

    def to_partner(source, target, sent, received):
        return pltpu.make_async_remote_copy(
            src_ref=source,
            dst_ref=target,
            send_sem=sent,
            recv_sem=received,
            device_id={"peer": to_peer},
            device_id_type=MESH,
        )

    raw = [
        to_partner(source, target, raw_send.at[k], raw_recv.at[k])
        for k, (source, target) in enumerate(
            (
                (tok_in.at[0], tok_theirs.at[span(me), :]),
                (gate_in.at[0, early_rows, :], weight_theirs.at[0]),
                (up_in.at[0, early_rows, :], weight_theirs.at[1]),
            )
        )
    ]
    for copy in raw:
        copy.start()

    def pass_dhid(origin):
        return to_partner(
            dhid.at[:, early_rows, span(origin)],
            dhid_theirs.at[:, :, span(origin)],
            dhid_send.at[origin],
            dhid_recv.at[origin],
        )

    def forward(origin):
        lanes = span(origin)
        half = rows // 2

        def some(i, carry):
            at = pl.ds(pl.multiple_of(i * half, half), half)
            gate = nt(wg[at, :], tok[lanes, :]) * in_scale
            upper = nt(wu[at, :], tok[lanes, :]) * in_scale
            dhidden = nt(wd[at, :], cot[lanes, :]) * hidden_scale
            sigma = jax.nn.sigmoid(gate)
            dhid[0, at, lanes] = (
                dhidden * upper * sigma * (1.0 + gate * (1.0 - sigma))
            ).astype(jnp.bfloat16)
            dhid[1, at, lanes] = (dhidden * gate * sigma).astype(jnp.bfloat16)
            return carry

        lax.fori_loop(0, 2, some, 0)
        pass_dhid(origin).start()

    for load in loads:
        load.wait()
    forward(me)

    def relay(step, arrays):
        left, right = me - 2 * step, me + 2 * step
        for a in arrays:
            @pl.when(z - step >= 0)
            def _():
                arrive(a, left)

                @pl.when(has_next)
                def _():
                    hop(a, left, 0).start()

                hop(a, left, 2).start()

            @pl.when(z + step < deep)
            def _():
                arrive(a, right)

                @pl.when(has_prev)
                def _():
                    hop(a, right, 1).start()

                hop(a, right, 2).start()

    def gather(step, arrays, use):
        left, right = me - 2 * step, me + 2 * step
        near_left, near_right = across - 2 * (step - 1), across + 2 * (step - 1)
        if step < deep:
            relay(step, arrays)
            if use is forward:
                if step == deep - 1:
                    raw[0].wait_recv()
                    first_hops(2, False)

                @pl.when(z - step >= 0)
                def _():
                    forward(left)

                @pl.when(z + step < deep)
                def _():
                    forward(right)

        @pl.when(z - step + 1 >= 0)
        def _():
            for a in arrays:
                arrive(a, near_left)
            use(near_left)

        if step > 1:
            @pl.when(z + step - 1 < deep)
            def _():
                for a in arrays:
                    arrive(a, near_right)
                use(near_right)

    for step in range(1, deep + 1):
        gather(step, (0, 1), forward)

    def rows_of(c):
        return pl.ds(pl.multiple_of(c * chunk, chunk), chunk)

    def exchange(c):
        return to_partner(own.at[c], landed.at[c], peer_send.at[c], peer_recv.at[c])

    def both(ref, at):
        return jnp.concatenate([ref[0, at, :], ref[1, at, :]], axis=0)

    def stepped(weight, terms, tokens):
        grad = jnp.dot(terms, tokens, preferred_element_type=jnp.float32) * in_scale
        return (weight.astype(jnp.float32) - RATE * grad).astype(jnp.bfloat16)

    def averaged(mine, theirs):
        return (
            (mine.astype(jnp.float32) + theirs.astype(jnp.float32)) * 0.5
        ).astype(jnp.bfloat16)

    def step_own(c):
        at = rows_of(c)
        weight = jnp.concatenate([wg[at, :], wu[at, :]], axis=0)
        own[c] = stepped(weight, both(dhid, at), tok[...])

    def late(c, carry):
        step_own(c)
        exchange(c).start()
        return carry

    def early(c, carry):
        step_own(c)
        return carry

    def unused(origin):
        pass

    begin = 0
    for step in range(1, deep + 1):
        end = -(-LATE * step // deep)
        lax.fori_loop(begin, end, late, 0)
        begin = end
        gather(step, (2,), unused)
    lax.fori_loop(LATE, CHUNKS, early, 0)

    def results(c, ref, at):
        return (
            pltpu.make_async_copy(
                ref.at[c, pl.ds(0, chunk), :], gate_out.at[0, at, :], out_sem.at[0, c]
            ),
            pltpu.make_async_copy(
                ref.at[c, pl.ds(chunk, chunk), :], up_out.at[0, at, :], out_sem.at[1, c]
            ),
        )

    raw[1].wait_recv()
    raw[2].wait_recv()

    def dhid_arrive(origin, carry):
        pass_dhid(origin).wait_recv()
        return carry

    lax.fori_loop(0, fsdp, dhid_arrive, 0)

    def early_average(c, carry):
        at = rows_of(c - LATE)
        theirs = stepped(both(weight_theirs, at), both(dhid_theirs, at), tok_theirs[...])
        own[c] = averaged(own[c], theirs)
        for copy in results(c, own, rows_of(c)):
            copy.start()
        return carry

    lax.fori_loop(LATE, CHUNKS, early_average, 0)

    def late_average(c, carry):
        exchange(c).wait_recv()
        landed[c] = averaged(own[c], landed[c])
        for copy in results(c, landed, rows_of(c)):
            copy.start()
        return carry

    lax.fori_loop(0, LATE, late_average, 0)

    def finish(ref):
        def one(c, carry):
            for copy in results(c, ref, rows_of(c)):
                copy.wait()
            return carry

        return one

    def sent(c, carry):
        exchange(c).wait_send()
        return carry

    def dhid_sent(origin, carry):
        pass_dhid(origin).wait_send()
        return carry

    lax.fori_loop(0, LATE, sent, 0)
    lax.fori_loop(0, fsdp, dhid_sent, 0)
    for copy in raw:
        copy.wait_send()

    for a in range(3):
        for step in range(deep):
            left, right = me - 2 * step, me + 2 * step

            @pl.when(z - step >= 0)
            def _():
                @pl.when(has_next)
                def _():
                    hop(a, left, 0).wait_send()

                hop(a, left, 2).wait_send()

            @pl.when(z + step < deep)
            def _():
                @pl.when(has_prev)
                def _():
                    hop(a, right, 1).wait_send()

                if step > 0:
                    hop(a, right, 2).wait_send()

    lax.fori_loop(LATE, CHUNKS, finish(own), 0)
    lax.fori_loop(0, LATE, finish(landed), 0)


def solution(mesh):
    fsdp, peers = mesh.shape["fsdp"], mesh.shape["peer"]

    def body(tokens, gate_weight, up_weight, down_weight, cotangent):
        _, part, width = tokens.shape
        rows = gate_weight.shape[1]
        every = part * fsdp
        chunk = rows // CHUNKS
        bf16 = jnp.bfloat16
        result = jax.ShapeDtypeStruct((1, rows, width), bf16)
        flops = 10 * every * rows * width
        return pl.pallas_call(
            functools.partial(kernel, fsdp, peers),
            out_shape=(result, result),
            in_specs=[pl.BlockSpec(memory_space=pl.ANY)] * 5,
            out_specs=(pl.BlockSpec(memory_space=pl.ANY),) * 2,
            scratch_shapes=[
                pltpu.VMEM((every, width), bf16),
                pltpu.VMEM((every, width), bf16),
                pltpu.VMEM((rows, width), bf16),
                pltpu.VMEM((rows, width), bf16),
                pltpu.VMEM((rows, width), bf16),
                pltpu.VMEM((every, width), bf16),
                pltpu.VMEM((2, rows, every), bf16),
                pltpu.VMEM((2, EARLY * chunk, every), bf16),
                pltpu.VMEM((2, EARLY * chunk, width), bf16),
                pltpu.VMEM((CHUNKS, 2 * chunk, width), bf16),
                pltpu.VMEM((LATE, 2 * chunk, width), bf16),
                pltpu.SemaphoreType.DMA((5,)),
                pltpu.SemaphoreType.DMA((3, fsdp, 3)),
                pltpu.SemaphoreType.DMA((3, fsdp)),
                pltpu.SemaphoreType.DMA((LATE,)),
                pltpu.SemaphoreType.DMA((LATE,)),
                pltpu.SemaphoreType.DMA((3,)),
                pltpu.SemaphoreType.DMA((3,)),
                pltpu.SemaphoreType.DMA((fsdp,)),
                pltpu.SemaphoreType.DMA((fsdp,)),
                pltpu.SemaphoreType.DMA((2, CHUNKS)),
            ],
            compiler_params=pltpu.CompilerParams(
                collective_id=0, has_side_effects=True, vmem_limit_bytes=56 * 2**20
            ),
            cost_estimate=pl.CostEstimate(
                flops=flops, bytes_accessed=10 * rows * width, transcendentals=every * rows
            ),
        )(tokens, gate_weight, up_weight, down_weight, cotangent)

    spec = P("peer", "fsdp", None)
    return jax.shard_map(
        body, mesh=mesh, in_specs=(spec,) * 5, out_specs=(spec, spec), check_vma=False
    )
```

```python
import functools

import jax
import jax.numpy as jnp
from jax import lax
from jax.experimental import pallas as pl
from jax.experimental.pallas import tpu as pltpu
from jax.sharding import PartitionSpec as P

HOP = 2
CHUNKS = 11
EARLY = 5
LATE = CHUNKS - EARLY
CROSS = 16
RATE = 1.0
MESH = pl.DeviceIdType.MESH


def nt(left, right):
    return lax.dot_general(
        left, right, (((1,), (1,)), ((), ())), preferred_element_type=jnp.float32
    )


def kernel(
    fsdp,
    peers,
    tok_in,
    gate_in,
    up_in,
    down_in,
    cot_in,
    gate_out,
    up_out,
    tok,
    cot,
    wg,
    wu,
    wd,
    tok_theirs,
    dhid,
    dhid_theirs,
    weight_theirs,
    gates,
    uppers,
    own,
    landed,
    load_sem,
    send_sem,
    recv_sem,
    peer_send,
    peer_recv,
    raw_send,
    raw_recv,
    dhid_send,
    dhid_recv,
    out_sem,
):
    part, width = tok_in.shape[1], tok_in.shape[2]
    rows = gate_in.shape[1]
    chunk = rows // CHUNKS
    in_scale = width ** (-0.5)
    hidden_scale = (rows * fsdp) ** (-0.5)
    deep = fsdp // 2

    me = lax.axis_index("fsdp")
    peer = lax.axis_index("peer")
    z, y = me // 2, me % 2
    across = z * 2 + 1 - y
    to_peer = lax.rem(peer + HOP, peers)
    from_peer = lax.rem(peer + peers - HOP, peers)
    has_prev, has_next = z > 0, z < deep - 1

    straight = part - CROSS
    pieces = (
        (tok_in, tok, 0, straight),
        (cot_in, cot, 0, straight),
        (tok_in, tok_theirs, 0, part),
        (tok_in, tok, straight, CROSS),
        (cot_in, cot, straight, CROSS),
    )
    early_rows = pl.ds(LATE * chunk, EARLY * chunk)

    loads = [
        pltpu.make_async_copy(source.at[0], target, load_sem.at[k])
        for k, (source, target) in enumerate(((gate_in, wg), (up_in, wu), (down_in, wd)))
    ]

    def span(origin):
        return pl.ds(pl.multiple_of(origin * part, part), part)

    loads += [
        pltpu.make_async_copy(source.at[0], target.at[span(me), :], load_sem.at[3 + a])
        for a, (source, target) in enumerate(((tok_in, tok), (cot_in, cot)))
    ]
    for load in reversed(loads):
        load.start()

    barrier = pltpu.get_barrier_semaphore()

    def greet(target):
        pl.semaphore_signal(barrier, inc=1, device_id=target, device_id_type=MESH)

    greet({"fsdp": across})
    greet({"peer": to_peer})
    greet({"peer": from_peer})

    @pl.when(has_prev)
    def _():
        greet({"fsdp": me - 2})

    @pl.when(has_next)
    def _():
        greet({"fsdp": me + 2})

    pl.semaphore_wait(barrier, 3 + has_prev.astype(jnp.int32) + has_next.astype(jnp.int32))

    def hop(a, origin, way, first=False):
        target = (me + 2, me - 2, across)[way]
        source, buffer, start, size = pieces[a]
        here = buffer.at[pl.ds(pl.multiple_of(origin * part + start, 16), size), :]
        return pltpu.make_async_remote_copy(
            src_ref=source.at[0, pl.ds(start, size), :] if first else here,
            dst_ref=here,
            send_sem=send_sem.at[a, origin, way],
            recv_sem=recv_sem.at[a, origin],
            device_id={"fsdp": target},
            device_id_type=MESH,
        )

    def arrive(a, origin):
        hop(a, origin, 2).wait_recv()

    def along(a, origin, first):
        @pl.when(has_next)
        def _():
            hop(a, origin, 0, first).start()

        @pl.when(has_prev)
        def _():
            hop(a, origin, 1, first).start()

    def first_hops(a, first):
        along(a, me, first)
        hop(a, me, 2, first).start()

    for a in (3, 4):
        hop(a, me, 2, True).start()
    for a in (0, 1):
        first_hops(a, True)
    for a in (3, 4):
        along(a, me, True)
    for a in (3, 4):
        arrive(a, across)
        along(a, across, False)

    def to_partner(source, target, sent, received):
        return pltpu.make_async_remote_copy(
            src_ref=source,
            dst_ref=target,
            send_sem=sent,
            recv_sem=received,
            device_id={"peer": to_peer},
            device_id_type=MESH,
        )

    raw = [
        to_partner(source, target, raw_send.at[k], raw_recv.at[k])
        for k, (source, target) in enumerate(
            (
                (tok_in.at[0], tok_theirs.at[span(me), :]),
                (gate_in.at[0, early_rows, :], weight_theirs.at[0]),
                (up_in.at[0, early_rows, :], weight_theirs.at[1]),
            )
        )
    ]
    for copy in raw:
        copy.start()

    def pass_dhid(origin):
        return to_partner(
            dhid.at[:, early_rows, span(origin)],
            dhid_theirs.at[:, :, span(origin)],
            dhid_send.at[origin],
            dhid_recv.at[origin],
        )

    half = rows // 2

    def half_at(i):
        return pl.ds(pl.multiple_of(i * half, half), half)

    def forward(origin, wait_tok, wait_cot):
        lanes = span(origin)

        def projections(i, carry):
            at = half_at(i)
            gates[at, :] = nt(wg[at, :], tok[lanes, :]) * in_scale
            uppers[at, :] = nt(wu[at, :], tok[lanes, :]) * in_scale
            return carry

        def hidden(i, carry):
            at = half_at(i)
            gate, upper = gates[at, :], uppers[at, :]
            dhidden = nt(wd[at, :], cot[lanes, :]) * hidden_scale
            sigma = jax.nn.sigmoid(gate)
            dhid[0, at, lanes] = (
                dhidden * upper * sigma * (1.0 + gate * (1.0 - sigma))
            ).astype(jnp.bfloat16)
            dhid[1, at, lanes] = (dhidden * gate * sigma).astype(jnp.bfloat16)
            return carry

        wait_tok()
        lax.fori_loop(0, 2, projections, 0)
        wait_cot()
        lax.fori_loop(0, 2, hidden, 0)
        pass_dhid(origin).start()

    def nothing():
        pass

    for load in loads:
        load.wait()
    forward(me, nothing, nothing)

    def relay(step, arrays):
        left, right = me - 2 * step, me + 2 * step
        for a in arrays:
            @pl.when(z - step >= 0)
            def _():
                arrive(a, left)

                @pl.when(has_next)
                def _():
                    hop(a, left, 0).start()

                hop(a, left, 2).start()

            @pl.when(z + step < deep)
            def _():
                arrive(a, right)

                @pl.when(has_prev)
                def _():
                    hop(a, right, 1).start()

                hop(a, right, 2).start()

    def relay_crossed(step):
        left, right = me - 2 * step, me + 2 * step
        far_left, far_right = across - 2 * step, across + 2 * step

        @pl.when(z - step >= 0)
        def _():
            for a, origin in ((3, left), (4, left), (3, far_left), (4, far_left)):
                arrive(a, origin)

                @pl.when(has_next)
                def _():
                    hop(a, origin, 0).start()

        @pl.when(z + step < deep)
        def _():
            for a, origin in ((3, right), (4, right), (3, far_right), (4, far_right)):
                arrive(a, origin)

                @pl.when(has_prev)
                def _():
                    hop(a, origin, 1).start()

    def near(step, use):
        near_left, near_right = across - 2 * (step - 1), across + 2 * (step - 1)

        @pl.when(z - step + 1 >= 0)
        def _():
            use(near_left)

        if step > 1:
            @pl.when(z + step - 1 < deep)
            def _():
                use(near_right)

    def forward_near(origin):
        forward(
            origin, functools.partial(arrive, 0, origin), functools.partial(arrive, 1, origin)
        )

    for step in range(1, deep + 1):
        if step < deep:
            relay(step, (0, 1))
            relay_crossed(step)
            if step == deep - 1:
                raw[0].wait_recv()
                first_hops(2, False)

            @pl.when(z - step >= 0)
            def _():
                forward(me - 2 * step, nothing, nothing)

            @pl.when(z + step < deep)
            def _():
                forward(me + 2 * step, nothing, nothing)

        near(step, forward_near)

    def rows_of(c):
        return pl.ds(pl.multiple_of(c * chunk, chunk), chunk)

    def exchange(c):
        return to_partner(own.at[c], landed.at[c], peer_send.at[c], peer_recv.at[c])

    def both(ref, at):
        return jnp.concatenate([ref[0, at, :], ref[1, at, :]], axis=0)

    def stepped(weight, terms, tokens):
        grad = jnp.dot(terms, tokens, preferred_element_type=jnp.float32) * in_scale
        return (weight.astype(jnp.float32) - RATE * grad).astype(jnp.bfloat16)

    def averaged(mine, theirs):
        return (
            (mine.astype(jnp.float32) + theirs.astype(jnp.float32)) * 0.5
        ).astype(jnp.bfloat16)

    def step_own(c):
        at = rows_of(c)
        weight = jnp.concatenate([wg[at, :], wu[at, :]], axis=0)
        own[c] = stepped(weight, both(dhid, at), tok[...])

    def late(c, carry):
        step_own(c)
        exchange(c).start()
        return carry

    def early(c, carry):
        step_own(c)
        return carry

    begin = 0
    for step in range(1, deep + 1):
        end = -(-LATE * step // deep)
        lax.fori_loop(begin, end, late, 0)
        begin = end
        if step < deep:
            relay(step, (2,))
        near(step, functools.partial(arrive, 2))
    lax.fori_loop(LATE, CHUNKS, early, 0)

    def results(c, ref, at):
        return (
            pltpu.make_async_copy(
                ref.at[c, pl.ds(0, chunk), :], gate_out.at[0, at, :], out_sem.at[0, c]
            ),
            pltpu.make_async_copy(
                ref.at[c, pl.ds(chunk, chunk), :], up_out.at[0, at, :], out_sem.at[1, c]
            ),
        )

    raw[1].wait_recv()
    raw[2].wait_recv()

    def dhid_arrive(origin, carry):
        pass_dhid(origin).wait_recv()
        return carry

    lax.fori_loop(0, fsdp, dhid_arrive, 0)

    def early_average(c, carry):
        at = rows_of(c - LATE)
        theirs = stepped(both(weight_theirs, at), both(dhid_theirs, at), tok_theirs[...])
        own[c] = averaged(own[c], theirs)
        for copy in results(c, own, rows_of(c)):
            copy.start()
        return carry

    lax.fori_loop(LATE, CHUNKS, early_average, 0)

    def late_average(c, carry):
        exchange(c).wait_recv()
        landed[c] = averaged(own[c], landed[c])
        for copy in results(c, landed, rows_of(c)):
            copy.start()
        return carry

    lax.fori_loop(0, LATE, late_average, 0)

    def finish(ref):
        def one(c, carry):
            for copy in results(c, ref, rows_of(c)):
                copy.wait()
            return carry

        return one

    def sent(c, carry):
        exchange(c).wait_send()
        return carry

    def dhid_sent(origin, carry):
        pass_dhid(origin).wait_send()
        return carry

    lax.fori_loop(0, LATE, sent, 0)
    lax.fori_loop(0, fsdp, dhid_sent, 0)
    for copy in raw:
        copy.wait_send()

    for a in range(3):
        for step in range(deep):
            left, right = me - 2 * step, me + 2 * step

            @pl.when(z - step >= 0)
            def _():
                @pl.when(has_next)
                def _():
                    hop(a, left, 0).wait_send()

                hop(a, left, 2).wait_send()

            @pl.when(z + step < deep)
            def _():
                @pl.when(has_prev)
                def _():
                    hop(a, right, 1).wait_send()

                if step > 0:
                    hop(a, right, 2).wait_send()

    for a in (3, 4):
        hop(a, me, 2).wait_send()
        for step in range(deep):
            @pl.when(has_next & (z - step >= 0))
            def _():
                hop(a, me - 2 * step, 0).wait_send()
                hop(a, across - 2 * step, 0).wait_send()

            @pl.when(has_prev & (z + step < deep))
            def _():
                hop(a, me + 2 * step, 1).wait_send()
                hop(a, across + 2 * step, 1).wait_send()

    lax.fori_loop(LATE, CHUNKS, finish(own), 0)
    lax.fori_loop(0, LATE, finish(landed), 0)


def solution(mesh):
    fsdp, peers = mesh.shape["fsdp"], mesh.shape["peer"]

    def body(tokens, gate_weight, up_weight, down_weight, cotangent):
        _, part, width = tokens.shape
        rows = gate_weight.shape[1]
        every = part * fsdp
        chunk = rows // CHUNKS
        bf16 = jnp.bfloat16
        result = jax.ShapeDtypeStruct((1, rows, width), bf16)
        flops = 10 * every * rows * width
        return pl.pallas_call(
            functools.partial(kernel, fsdp, peers),
            out_shape=(result, result),
            in_specs=[pl.BlockSpec(memory_space=pl.ANY)] * 5,
            out_specs=(pl.BlockSpec(memory_space=pl.ANY),) * 2,
            scratch_shapes=[
                pltpu.VMEM((every, width), bf16),
                pltpu.VMEM((every, width), bf16),
                pltpu.VMEM((rows, width), bf16),
                pltpu.VMEM((rows, width), bf16),
                pltpu.VMEM((rows, width), bf16),
                pltpu.VMEM((every, width), bf16),
                pltpu.VMEM((2, rows, every), bf16),
                pltpu.VMEM((2, EARLY * chunk, every), bf16),
                pltpu.VMEM((2, EARLY * chunk, width), bf16),
                pltpu.VMEM((rows, part), jnp.float32),
                pltpu.VMEM((rows, part), jnp.float32),
                pltpu.VMEM((CHUNKS, 2 * chunk, width), bf16),
                pltpu.VMEM((LATE, 2 * chunk, width), bf16),
                pltpu.SemaphoreType.DMA((5,)),
                pltpu.SemaphoreType.DMA((5, fsdp, 3)),
                pltpu.SemaphoreType.DMA((5, fsdp)),
                pltpu.SemaphoreType.DMA((LATE,)),
                pltpu.SemaphoreType.DMA((LATE,)),
                pltpu.SemaphoreType.DMA((3,)),
                pltpu.SemaphoreType.DMA((3,)),
                pltpu.SemaphoreType.DMA((fsdp,)),
                pltpu.SemaphoreType.DMA((fsdp,)),
                pltpu.SemaphoreType.DMA((2, CHUNKS)),
            ],
            compiler_params=pltpu.CompilerParams(
                collective_id=0, has_side_effects=True, vmem_limit_bytes=46 * 2**20
            ),
            cost_estimate=pl.CostEstimate(
                flops=flops, bytes_accessed=10 * rows * width, transcendentals=every * rows
            ),
        )(tokens, gate_weight, up_weight, down_weight, cotangent)

    spec = P("peer", "fsdp", None)
    return jax.shard_map(
        body, mesh=mesh, in_specs=(spec,) * 5, out_specs=(spec, spec), check_vma=False
    )
```

```python
import functools

import jax
import jax.numpy as jnp
from jax import lax
from jax.experimental import pallas as pl
from jax.experimental.pallas import tpu as pltpu
from jax.sharding import PartitionSpec as P

HOP = 2
CHUNKS = 11
EARLY = 5
LATE = CHUNKS - EARLY
COLUMNS = 512
RATE = 1.0
MESH = pl.DeviceIdType.MESH


def nt(left, right):
    return lax.dot_general(
        left, right, (((1,), (1,)), ((), ())), preferred_element_type=jnp.float32
    )


def kernel(
    fsdp,
    peers,
    tok_in,
    gate_in,
    up_in,
    down_in,
    cot_in,
    gate_out,
    up_out,
    tok,
    cot,
    wg,
    wu,
    wd,
    tok_theirs,
    dhid,
    dhid_theirs,
    weight_theirs,
    gates,
    uppers,
    settled,
    own,
    landed,
    load_sem,
    send_sem,
    recv_sem,
    peer_send,
    peer_recv,
    raw_send,
    raw_recv,
    dhid_send,
    dhid_recv,
    out_sem,
):
    part, width = tok_in.shape[1], tok_in.shape[2]
    rows = gate_in.shape[1]
    chunk = rows // CHUNKS
    in_scale = width ** (-0.5)
    hidden_scale = (rows * fsdp) ** (-0.5)
    deep = fsdp // 2

    me = lax.axis_index("fsdp")
    peer = lax.axis_index("peer")
    z, y = me // 2, me % 2
    across = z * 2 + 1 - y
    to_peer = lax.rem(peer + HOP, peers)
    from_peer = lax.rem(peer + peers - HOP, peers)
    has_prev, has_next = z > 0, z < deep - 1

    pieces = ((tok_in, tok), (cot_in, cot), (tok_in, tok_theirs))
    early_rows = pl.ds(LATE * chunk, EARLY * chunk)

    loads = [
        pltpu.make_async_copy(source.at[0], target, load_sem.at[k])
        for k, (source, target) in enumerate(((gate_in, wg), (up_in, wu), (down_in, wd)))
    ]

    def span(origin):
        return pl.ds(pl.multiple_of(origin * part, part), part)

    loads += [
        pltpu.make_async_copy(source.at[0], target.at[span(me), :], load_sem.at[3 + a])
        for a, (source, target) in enumerate(((tok_in, tok), (cot_in, cot)))
    ]
    for load in reversed(loads):
        load.start()

    barrier = pltpu.get_barrier_semaphore()

    def greet(target):
        pl.semaphore_signal(barrier, inc=1, device_id=target, device_id_type=MESH)

    greet({"fsdp": across})
    greet({"peer": to_peer})
    greet({"peer": from_peer})

    @pl.when(has_prev)
    def _():
        greet({"fsdp": me - 2})

    @pl.when(has_next)
    def _():
        greet({"fsdp": me + 2})

    pl.semaphore_wait(barrier, 3 + has_prev.astype(jnp.int32) + has_next.astype(jnp.int32))

    def hop(a, origin, way, first=False):
        target = (me + 2, me - 2, across)[way]
        source, buffer = pieces[a]
        here = buffer.at[span(origin), :]
        return pltpu.make_async_remote_copy(
            src_ref=source.at[0] if first else here,
            dst_ref=here,
            send_sem=send_sem.at[a, origin, way],
            recv_sem=recv_sem.at[a, origin],
            device_id={"fsdp": target},
            device_id_type=MESH,
        )

    def arrive(a, origin):
        hop(a, origin, 2).wait_recv()

    def first_hops(a, first):
        @pl.when(has_next)
        def _():
            hop(a, me, 0, first).start()

        @pl.when(has_prev)
        def _():
            hop(a, me, 1, first).start()

        hop(a, me, 2, first).start()

    for a in (0, 1):
        first_hops(a, True)

    def to_partner(source, target, sent, received):
        return pltpu.make_async_remote_copy(
            src_ref=source,
            dst_ref=target,
            send_sem=sent,
            recv_sem=received,
            device_id={"peer": to_peer},
            device_id_type=MESH,
        )

    raw = [
        to_partner(source, target, raw_send.at[k], raw_recv.at[k])
        for k, (source, target) in enumerate(
            (
                (tok_in.at[0], tok_theirs.at[span(me), :]),
                (gate_in.at[0, early_rows, :], weight_theirs.at[0]),
                (up_in.at[0, early_rows, :], weight_theirs.at[1]),
            )
        )
    ]
    for copy in raw:
        copy.start()

    def pair(layer):
        return pl.ds(pl.multiple_of(layer * 2 * part, 2 * part), 2 * part)

    def pass_dhid(layer):
        return to_partner(
            dhid.at[:, early_rows, pair(layer)],
            dhid_theirs.at[:, :, pair(layer)],
            dhid_send.at[layer],
            dhid_recv.at[layer],
        )

    half = rows // 2

    def half_at(i):
        return pl.ds(pl.multiple_of(i * half, half), half)

    def forward(layer):
        lanes = pair(layer)
        other = layer * 2 + 1 - y

        def projections(i, carry):
            at = half_at(i)
            gates[at, :] = nt(wg[at, :], tok[lanes, :]) * in_scale
            uppers[at, :] = nt(wu[at, :], tok[lanes, :]) * in_scale
            return carry

        def hidden(i, carry):
            at = half_at(i)
            gate, upper = gates[at, :], uppers[at, :]
            dhidden = nt(wd[at, :], cot[lanes, :]) * hidden_scale
            sigma = jax.nn.sigmoid(gate)
            dhid[0, at, lanes] = (
                dhidden * upper * sigma * (1.0 + gate * (1.0 - sigma))
            ).astype(jnp.bfloat16)
            dhid[1, at, lanes] = (dhidden * gate * sigma).astype(jnp.bfloat16)
            return carry

        arrive(0, other)
        lax.fori_loop(0, 2, projections, 0)
        arrive(1, other)
        lax.fori_loop(0, 2, hidden, 0)
        pass_dhid(layer).start()

    for load in loads:
        load.wait()

    def relay(step, arrays):
        left, right = me - 2 * step, me + 2 * step
        for a in arrays:
            @pl.when(z - step >= 0)
            def _():
                arrive(a, left)

                @pl.when(has_next)
                def _():
                    hop(a, left, 0).start()

                hop(a, left, 2).start()

            @pl.when(z + step < deep)
            def _():
                arrive(a, right)

                @pl.when(has_prev)
                def _():
                    hop(a, right, 1).start()

                hop(a, right, 2).start()

    def near(step, use):
        @pl.when(z - step + 1 >= 0)
        def _():
            use(z - step + 1)

        if step > 1:
            @pl.when(z + step - 1 < deep)
            def _():
                use(z + step - 1)

    for step in range(1, deep + 1):
        if step < deep:
            relay(step, (0, 1))
            if step == deep - 1:
                raw[0].wait_recv()
                first_hops(2, False)
        near(step, forward)

    def rows_of(c):
        return pl.ds(pl.multiple_of(c * chunk, chunk), chunk)

    def exchange(c):
        return to_partner(own.at[c], landed.at[c], peer_send.at[c], peer_recv.at[c])

    def stepped(weight, terms, tokens):
        grad = jnp.dot(terms, tokens, preferred_element_type=jnp.float32) * in_scale
        return (weight.astype(jnp.float32) - RATE * grad).astype(jnp.bfloat16)

    def averaged(mine, theirs):
        return (
            (mine.astype(jnp.float32) + theirs.astype(jnp.float32)) * 0.5
        ).astype(jnp.bfloat16)

    def step_own(c):
        at = rows_of(c)
        weight = jnp.concatenate([wg[at, :], wu[at, :]], axis=0)
        terms = jnp.concatenate([dhid[0, at, :], dhid[1, at, :]], axis=0)
        own[c] = stepped(weight, terms, tok[...])

    def late(c, carry):
        step_own(c)
        exchange(c).start()
        return carry

    def columns(i):
        return pl.ds(pl.multiple_of(i * COLUMNS, COLUMNS), COLUMNS)

    def early(i, carry):
        cols = columns(i)
        for k, weight in enumerate((wg, wu)):
            settled[k, :, cols] = stepped(
                weight[early_rows, cols], dhid[k, early_rows, :], tok[:, cols]
            )
        return carry

    begin = 0
    for step in range(1, deep + 1):
        end = -(-LATE * step // deep)
        lax.fori_loop(begin, end, late, 0)
        begin = end
        if step < deep:
            relay(step, (2,))
        near(step, lambda layer: arrive(2, layer * 2 + 1 - y))
    lax.fori_loop(0, width // COLUMNS, early, 0)

    def results(c):
        at = rows_of(c)
        return (
            pltpu.make_async_copy(
                landed.at[c, pl.ds(0, chunk), :], gate_out.at[0, at, :], out_sem.at[0, c]
            ),
            pltpu.make_async_copy(
                landed.at[c, pl.ds(chunk, chunk), :], up_out.at[0, at, :], out_sem.at[1, c]
            ),
        )

    early_results = [
        pltpu.make_async_copy(settled.at[k], out.at[0, early_rows, :], out_sem.at[k, LATE])
        for k, out in enumerate((gate_out, up_out))
    ]

    raw[1].wait_recv()
    raw[2].wait_recv()

    def dhid_arrive(layer, carry):
        pass_dhid(layer).wait_recv()
        return carry

    lax.fori_loop(0, deep, dhid_arrive, 0)

    def early_average(i, carry):
        cols = columns(i)
        for k in range(2):
            theirs = stepped(weight_theirs[k, :, cols], dhid_theirs[k], tok_theirs[:, cols])
            settled[k, :, cols] = averaged(settled[k, :, cols], theirs)
        return carry

    lax.fori_loop(0, width // COLUMNS, early_average, 0)
    for copy in early_results:
        copy.start()

    def late_average(c, carry):
        exchange(c).wait_recv()
        landed[c] = averaged(own[c], landed[c])
        for copy in results(c):
            copy.start()
        return carry

    lax.fori_loop(0, LATE, late_average, 0)

    def finish(c, carry):
        for copy in results(c):
            copy.wait()
        return carry

    def sent(c, carry):
        exchange(c).wait_send()
        return carry

    def dhid_sent(layer, carry):
        pass_dhid(layer).wait_send()
        return carry

    lax.fori_loop(0, LATE, sent, 0)
    lax.fori_loop(0, deep, dhid_sent, 0)
    for copy in raw:
        copy.wait_send()

    for a in range(3):
        for step in range(deep):
            left, right = me - 2 * step, me + 2 * step

            @pl.when(z - step >= 0)
            def _():
                @pl.when(has_next)
                def _():
                    hop(a, left, 0).wait_send()

                hop(a, left, 2).wait_send()

            @pl.when(z + step < deep)
            def _():
                @pl.when(has_prev)
                def _():
                    hop(a, right, 1).wait_send()

                if step > 0:
                    hop(a, right, 2).wait_send()

    for copy in early_results:
        copy.wait()
    lax.fori_loop(0, LATE, finish, 0)


def solution(mesh):
    fsdp, peers = mesh.shape["fsdp"], mesh.shape["peer"]

    def body(tokens, gate_weight, up_weight, down_weight, cotangent):
        _, part, width = tokens.shape
        rows = gate_weight.shape[1]
        every = part * fsdp
        chunk = rows // CHUNKS
        bf16 = jnp.bfloat16
        result = jax.ShapeDtypeStruct((1, rows, width), bf16)
        flops = 10 * every * rows * width
        return pl.pallas_call(
            functools.partial(kernel, fsdp, peers),
            out_shape=(result, result),
            in_specs=[pl.BlockSpec(memory_space=pltpu.HBM)] * 5,
            out_specs=(pl.BlockSpec(memory_space=pl.ANY),) * 2,
            scratch_shapes=[
                pltpu.VMEM((every, width), bf16),
                pltpu.VMEM((every, width), bf16),
                pltpu.VMEM((rows, width), bf16),
                pltpu.VMEM((rows, width), bf16),
                pltpu.VMEM((rows, width), bf16),
                pltpu.VMEM((every, width), bf16),
                pltpu.VMEM((2, rows, every), bf16),
                pltpu.VMEM((2, EARLY * chunk, every), bf16),
                pltpu.VMEM((2, EARLY * chunk, width), bf16),
                pltpu.VMEM((rows, 2 * part), jnp.float32),
                pltpu.VMEM((rows, 2 * part), jnp.float32),
                pltpu.VMEM((2, EARLY * chunk, width), bf16),
                pltpu.VMEM((LATE, 2 * chunk, width), bf16),
                pltpu.VMEM((LATE, 2 * chunk, width), bf16),
                pltpu.SemaphoreType.DMA((5,)),
                pltpu.SemaphoreType.DMA((3, fsdp, 3)),
                pltpu.SemaphoreType.DMA((3, fsdp)),
                pltpu.SemaphoreType.DMA((LATE,)),
                pltpu.SemaphoreType.DMA((LATE,)),
                pltpu.SemaphoreType.DMA((3,)),
                pltpu.SemaphoreType.DMA((3,)),
                pltpu.SemaphoreType.DMA((fsdp // 2,)),
                pltpu.SemaphoreType.DMA((fsdp // 2,)),
                pltpu.SemaphoreType.DMA((2, LATE + 1)),
            ],
            compiler_params=pltpu.CompilerParams(
                collective_id=0, has_side_effects=True, vmem_limit_bytes=46 * 2**20
            ),
            cost_estimate=pl.CostEstimate(
                flops=flops, bytes_accessed=10 * rows * width, transcendentals=every * rows
            ),
        )(tokens, gate_weight, up_weight, down_weight, cotangent)

    spec = P("peer", "fsdp", None)
    return jax.shard_map(
        body, mesh=mesh, in_specs=(spec,) * 5, out_specs=(spec, spec), check_vma=False
    )
```

```python
import functools

import jax
import jax.numpy as jnp
from jax import lax
from jax.experimental import pallas as pl
from jax.experimental.pallas import tpu as pltpu
from jax.sharding import PartitionSpec as P

HOP = 2
CHUNKS = 11
EARLY = 6
LATE = CHUNKS - EARLY
COLUMNS = 512
RATE = 1.0
MESH = pl.DeviceIdType.MESH


def nt(left, right):
    return lax.dot_general(
        left, right, (((1,), (1,)), ((), ())), preferred_element_type=jnp.float32
    )


def kernel(
    fsdp,
    peers,
    tok_in,
    gate_in,
    up_in,
    down_in,
    cot_in,
    gate_out,
    up_out,
    tok,
    cot,
    wg,
    wu,
    wd,
    tok_theirs,
    dhid,
    dhid_theirs,
    weight_theirs,
    gates,
    uppers,
    settled,
    own,
    landed,
    load_sem,
    send_sem,
    recv_sem,
    peer_send,
    peer_recv,
    raw_send,
    raw_recv,
    dhid_send,
    dhid_recv,
    out_sem,
):
    part, width = tok_in.shape[1], tok_in.shape[2]
    rows = gate_in.shape[1]
    chunk = rows // CHUNKS
    in_scale = width ** (-0.5)
    hidden_scale = (rows * fsdp) ** (-0.5)
    deep = fsdp // 2

    me = lax.axis_index("fsdp")
    peer = lax.axis_index("peer")
    z, y = me // 2, me % 2
    across = z * 2 + 1 - y
    to_peer = lax.rem(peer + HOP, peers)
    from_peer = lax.rem(peer + peers - HOP, peers)
    has_prev, has_next = z > 0, z < deep - 1

    pieces = ((tok_in, tok), (cot_in, cot), (tok_in, tok_theirs))
    early_rows = pl.ds(LATE * chunk, EARLY * chunk)

    loads = [
        pltpu.make_async_copy(source.at[0], target, load_sem.at[k])
        for k, (source, target) in enumerate(((gate_in, wg), (up_in, wu), (down_in, wd)))
    ]

    def span(origin):
        return pl.ds(pl.multiple_of(origin * part, part), part)

    loads += [
        pltpu.make_async_copy(source.at[0], target.at[span(me), :], load_sem.at[3 + a])
        for a, (source, target) in enumerate(((tok_in, tok), (cot_in, cot)))
    ]
    for load in reversed(loads):
        load.start()

    barrier = pltpu.get_barrier_semaphore()

    def greet(target):
        pl.semaphore_signal(barrier, inc=1, device_id=target, device_id_type=MESH)

    greet({"fsdp": across})
    greet({"peer": to_peer})
    greet({"peer": from_peer})

    @pl.when(has_prev)
    def _():
        greet({"fsdp": me - 2})

    @pl.when(has_next)
    def _():
        greet({"fsdp": me + 2})

    pl.semaphore_wait(barrier, 3 + has_prev.astype(jnp.int32) + has_next.astype(jnp.int32))

    def hop(a, origin, way, first=False):
        target = (me + 2, me - 2, across)[way]
        source, buffer = pieces[a]
        here = buffer.at[span(origin), :]
        return pltpu.make_async_remote_copy(
            src_ref=source.at[0] if first else here,
            dst_ref=here,
            send_sem=send_sem.at[a, origin, way],
            recv_sem=recv_sem.at[a, origin],
            device_id={"fsdp": target},
            device_id_type=MESH,
        )

    def arrive(a, origin):
        hop(a, origin, 2).wait_recv()

    def first_hops(a, first):
        @pl.when(has_next)
        def _():
            hop(a, me, 0, first).start()

        @pl.when(has_prev)
        def _():
            hop(a, me, 1, first).start()

        hop(a, me, 2, first).start()

    for a in (0, 1):
        first_hops(a, True)

    def to_partner(source, target, sent, received):
        return pltpu.make_async_remote_copy(
            src_ref=source,
            dst_ref=target,
            send_sem=sent,
            recv_sem=received,
            device_id={"peer": to_peer},
            device_id_type=MESH,
        )

    raw = [
        to_partner(source, target, raw_send.at[k], raw_recv.at[k])
        for k, (source, target) in enumerate(
            (
                (tok_in.at[0], tok_theirs.at[span(me), :]),
                (gate_in.at[0, early_rows, :], weight_theirs.at[0]),
                (up_in.at[0, early_rows, :], weight_theirs.at[1]),
            )
        )
    ]
    for copy in raw:
        copy.start()

    def pair(layer):
        return pl.ds(pl.multiple_of(layer * 2 * part, 2 * part), 2 * part)

    def pass_dhid(layer):
        return to_partner(
            dhid.at[:, early_rows, pair(layer)],
            dhid_theirs.at[:, :, pair(layer)],
            dhid_send.at[layer],
            dhid_recv.at[layer],
        )

    half = rows // 2

    def half_at(i):
        return pl.ds(pl.multiple_of(i * half, half), half)

    def forward(layer):
        lanes = pair(layer)
        other = layer * 2 + 1 - y

        def projections(i, carry):
            at = half_at(i)
            gates[at, :] = nt(wg[at, :], tok[lanes, :]) * in_scale
            uppers[at, :] = nt(wu[at, :], tok[lanes, :]) * in_scale
            return carry

        def hidden(i, carry):
            at = half_at(i)
            gate, upper = gates[at, :], uppers[at, :]
            dhidden = nt(wd[at, :], cot[lanes, :]) * hidden_scale
            sigma = jax.nn.sigmoid(gate)
            dhid[0, at, lanes] = (
                dhidden * upper * sigma * (1.0 + gate * (1.0 - sigma))
            ).astype(jnp.bfloat16)
            dhid[1, at, lanes] = (dhidden * gate * sigma).astype(jnp.bfloat16)
            return carry

        arrive(0, other)
        lax.fori_loop(0, 2, projections, 0)
        arrive(1, other)
        lax.fori_loop(0, 2, hidden, 0)
        pass_dhid(layer).start()

    for load in loads:
        load.wait()

    def relay(step, arrays):
        left, right = me - 2 * step, me + 2 * step
        for a in arrays:
            @pl.when(z - step >= 0)
            def _():
                arrive(a, left)

                @pl.when(has_next)
                def _():
                    hop(a, left, 0).start()

                hop(a, left, 2).start()

            @pl.when(z + step < deep)
            def _():
                arrive(a, right)

                @pl.when(has_prev)
                def _():
                    hop(a, right, 1).start()

                hop(a, right, 2).start()

    def near(step, use):
        @pl.when(z - step + 1 >= 0)
        def _():
            use(z - step + 1)

        if step > 1:
            @pl.when(z + step - 1 < deep)
            def _():
                use(z + step - 1)

    for step in range(1, deep + 1):
        if step < deep:
            relay(step, (0, 1))
            if step == deep - 1:
                raw[0].wait_recv()
                first_hops(2, False)
        near(step, forward)

    def rows_of(c):
        return pl.ds(pl.multiple_of(c * chunk, chunk), chunk)

    def exchange(c):
        return to_partner(own.at[c], landed.at[c], peer_send.at[c], peer_recv.at[c])

    def stepped(weight, terms, tokens):
        grad = jnp.dot(terms, tokens, preferred_element_type=jnp.float32) * in_scale
        return (weight.astype(jnp.float32) - RATE * grad).astype(jnp.bfloat16)

    def averaged(mine, theirs):
        return (
            (mine.astype(jnp.float32) + theirs.astype(jnp.float32)) * 0.5
        ).astype(jnp.bfloat16)

    def step_own(c):
        at = rows_of(c)
        weight = jnp.concatenate([wg[at, :], wu[at, :]], axis=0)
        terms = jnp.concatenate([dhid[0, at, :], dhid[1, at, :]], axis=0)
        own[c] = stepped(weight, terms, tok[...])

    def late(c, carry):
        step_own(c)
        exchange(c).start()
        return carry

    def columns(i):
        return pl.ds(pl.multiple_of(i * COLUMNS, COLUMNS), COLUMNS)

    def early(i, carry):
        cols = columns(i)
        for k, weight in enumerate((wg, wu)):
            settled[k, :, cols] = stepped(
                weight[early_rows, cols], dhid[k, early_rows, :], tok[:, cols]
            )
        return carry

    begin = 0
    for step in range(1, deep + 1):
        end = -(-LATE * step // deep)
        lax.fori_loop(begin, end, late, 0)
        begin = end
        if step < deep:
            relay(step, (2,))
        near(step, lambda layer: arrive(2, layer * 2 + 1 - y))
    lax.fori_loop(0, width // COLUMNS, early, 0)

    def results(c):
        at = rows_of(c)
        return (
            pltpu.make_async_copy(
                landed.at[c, pl.ds(0, chunk), :], gate_out.at[0, at, :], out_sem.at[0, c]
            ),
            pltpu.make_async_copy(
                landed.at[c, pl.ds(chunk, chunk), :], up_out.at[0, at, :], out_sem.at[1, c]
            ),
        )

    early_results = [
        pltpu.make_async_copy(settled.at[k], out.at[0, early_rows, :], out_sem.at[k, LATE])
        for k, out in enumerate((gate_out, up_out))
    ]

    raw[1].wait_recv()
    raw[2].wait_recv()

    def dhid_arrive(layer, carry):
        pass_dhid(layer).wait_recv()
        return carry

    lax.fori_loop(0, deep, dhid_arrive, 0)

    def early_average(i, carry):
        cols = columns(i)
        for k in range(2):
            theirs = stepped(weight_theirs[k, :, cols], dhid_theirs[k], tok_theirs[:, cols])
            settled[k, :, cols] = averaged(settled[k, :, cols], theirs)
        return carry

    lax.fori_loop(0, width // COLUMNS, early_average, 0)
    for copy in early_results:
        copy.start()

    def late_average(c, carry):
        exchange(c).wait_recv()
        landed[c] = averaged(own[c], landed[c])
        for copy in results(c):
            copy.start()
        return carry

    lax.fori_loop(0, LATE, late_average, 0)

    def finish(c, carry):
        for copy in results(c):
            copy.wait()
        return carry

    def sent(c, carry):
        exchange(c).wait_send()
        return carry

    def dhid_sent(layer, carry):
        pass_dhid(layer).wait_send()
        return carry

    lax.fori_loop(0, LATE, sent, 0)
    lax.fori_loop(0, deep, dhid_sent, 0)
    for copy in raw:
        copy.wait_send()

    for a in range(3):
        for step in range(deep):
            left, right = me - 2 * step, me + 2 * step

            @pl.when(z - step >= 0)
            def _():
                @pl.when(has_next)
                def _():
                    hop(a, left, 0).wait_send()

                hop(a, left, 2).wait_send()

            @pl.when(z + step < deep)
            def _():
                @pl.when(has_prev)
                def _():
                    hop(a, right, 1).wait_send()

                if step > 0:
                    hop(a, right, 2).wait_send()

    for copy in early_results:
        copy.wait()
    lax.fori_loop(0, LATE, finish, 0)


def solution(mesh):
    fsdp, peers = mesh.shape["fsdp"], mesh.shape["peer"]

    def body(tokens, gate_weight, up_weight, down_weight, cotangent):
        _, part, width = tokens.shape
        rows = gate_weight.shape[1]
        every = part * fsdp
        chunk = rows // CHUNKS
        bf16 = jnp.bfloat16
        result = jax.ShapeDtypeStruct((1, rows, width), bf16)
        flops = 10 * every * rows * width
        return pl.pallas_call(
            functools.partial(kernel, fsdp, peers),
            out_shape=(result, result),
            in_specs=[pl.BlockSpec(memory_space=pltpu.HBM)] * 5,
            out_specs=(pl.BlockSpec(memory_space=pl.ANY),) * 2,
            scratch_shapes=[
                pltpu.VMEM((every, width), bf16),
                pltpu.VMEM((every, width), bf16),
                pltpu.VMEM((rows, width), bf16),
                pltpu.VMEM((rows, width), bf16),
                pltpu.VMEM((rows, width), bf16),
                pltpu.VMEM((every, width), bf16),
                pltpu.VMEM((2, rows, every), bf16),
                pltpu.VMEM((2, EARLY * chunk, every), bf16),
                pltpu.VMEM((2, EARLY * chunk, width), bf16),
                pltpu.VMEM((rows, 2 * part), jnp.float32),
                pltpu.VMEM((rows, 2 * part), jnp.float32),
                pltpu.VMEM((2, EARLY * chunk, width), bf16),
                pltpu.VMEM((LATE, 2 * chunk, width), bf16),
                pltpu.VMEM((LATE, 2 * chunk, width), bf16),
                pltpu.SemaphoreType.DMA((5,)),
                pltpu.SemaphoreType.DMA((3, fsdp, 3)),
                pltpu.SemaphoreType.DMA((3, fsdp)),
                pltpu.SemaphoreType.DMA((LATE,)),
                pltpu.SemaphoreType.DMA((LATE,)),
                pltpu.SemaphoreType.DMA((3,)),
                pltpu.SemaphoreType.DMA((3,)),
                pltpu.SemaphoreType.DMA((fsdp // 2,)),
                pltpu.SemaphoreType.DMA((fsdp // 2,)),
                pltpu.SemaphoreType.DMA((2, LATE + 1)),
            ],
            compiler_params=pltpu.CompilerParams(
                collective_id=0, has_side_effects=True, vmem_limit_bytes=46 * 2**20
            ),
            cost_estimate=pl.CostEstimate(
                flops=flops, bytes_accessed=10 * rows * width, transcendentals=every * rows
            ),
        )(tokens, gate_weight, up_weight, down_weight, cotangent)

    spec = P("peer", "fsdp", None)
    return jax.shard_map(
        body, mesh=mesh, in_specs=(spec,) * 5, out_specs=(spec, spec), check_vma=False
    )
```
